32 devices in a mesh: groups: 2 (over y), tm: 8 (over z, x), space: 2 (over core).
Axes of the slice: x: 2, y: 2, z: 4, core: 2. Of those that a mesh axis runs over, the one named last changes fastest.
Arguments:
- interior_diag: bfloat16 [24576, 1536], P(('groups', 'tm'), 'space'), parts along dimension 0, may hold values from -1 to 5, as said below
- coupling: bfloat16 [24576, 1536], P(('groups', 'tm'), 'space'), parts along dimension 0, may hold values from -0.29882812 to 0.29882812
- arrow_rows: bfloat16 [12288, 1536], P(('groups', 'tm', 'space')), parts along dimension 0, may hold values from -0.59765625 to 0.59765625
- separator_diag: bfloat16 [24576, 1536], P(('groups', 'tm'), 'space'), parts along dimension 0, may hold values from -1 to 5, as said below
- tip: bfloat16 [1536, 768], P('groups', 'space'), parts along dimension 0, may hold values from -6 to 6
- lengths: int32 [16], P('groups'), parts along dimension 0, may hold values from 1 to 2, 12 in all
Outputs:
- new_separator: bfloat16 [24576, 1536], P(('groups', 'tm'), 'space'), parts along dimension 0
- arrow_fill: bfloat16 [12288, 1536], P(('groups', 'tm'), 'space'), parts along dimension 0
- new_tip: float32 [1536, 768], P('groups', 'space'), parts along dimension 0
The draws below stay inside these ranges and needn't reach their ends.
There are 2 independent parts, one for each index of `groups`. The reference program is written for one: setup_inputs(seed, part) draws one part's arguments, and reference() takes and returns one part's arrays. A program takes and returns all parts, laid end to end along the dimension named above; each array names one. Nothing has to cross between parts.
Inputs may be any that keep to these rules, and one draw needn't show every extreme that they name: `interior_diag`: each block of 1536 rows is symmetric with eigenvalues above 0.5. `separator_diag`: each block of 1536 rows is symmetric with eigenvalues above 0.5. `lengths`: partition p has an interior block exactly when entry p is 2; some entry is 2.
All inputs are finite; a program needn't handle non-finite values.
Results may differ from the reference program's by a relative error of at most 0.008.
Values may be sent and summed in bfloat16 or wider, within the bound.
A program may use at most 128 MiB of HBM per device.

```python
import math
import jax
import jax.numpy as jnp
import numpy as np
from jax import lax

B = 1536
A = 768
PARTITIONS = 8


def spd_blocks(key):
    noise_key, center_key = jax.random.split(key)
    noise_draw = jax.random.normal(noise_key, (PARTITIONS, B, B), jnp.float32)
    symmetric = (noise_draw + jnp.swapaxes(noise_draw, 1, 2)) * (0.5 / math.sqrt(B))
    center = jax.random.uniform(center_key, (PARTITIONS, B), jnp.float32, 2.0, 4.0)
    identity = jnp.eye(B, dtype=jnp.float32)
    return (symmetric + center[:, :, None] * identity[None, :, :]).reshape(PARTITIONS * B, B)


def draw_interior_diag(key, part):
    return spd_blocks(jax.random.fold_in(key, 11)).astype(jnp.bfloat16)


def draw_separator_diag(key, part):
    return spd_blocks(jax.random.fold_in(key, 23)).astype(jnp.bfloat16)


def steps_of(own_key, extent, cuts, low, high):
    def one(dim, parts):
        heights = jax.random.uniform(jax.random.fold_in(jax.random.fold_in(own_key, 6), dim), (parts,), jnp.float32, low / len(cuts), high / len(cuts))
        return jnp.repeat(jnp.exp(heights), extent[dim] // parts).reshape((-1,) + (1,) * (len(extent) - dim - 1))

    level = one(*cuts[0])
    for cut in cuts[1:]:
        level = level * one(*cut)
    return level


def profile(count, total, most, lean):
    weights = [(1 << 20) // math.isqrt(rank ** lean) + 1 for rank in range(2, count + 1)]
    rest, given = total - most - (count - 1), [1] * (count - 1)
    while rest > 0:
        candidates = [i for i in range(count - 1) if given[i] < most]
        mass, remaining = sum([weights[i] for i in candidates]), rest
        for i in candidates:
            extra = min(most - given[i], max(1, remaining * weights[i] // mass), rest)
            given[i] = given[i] + extra
            rest = rest - extra
    return np.array([most] + given)


def ragged(rng, number_of, total, most, skew):
    if number_of == 2:
        one = jax.random.randint(rng, (), max(1, total - most), min(most, total - 1) + 1)
        return jnp.stack([one, total - one])
    sizes = jnp.asarray(profile(number_of, total, most, skew), jnp.int32)
    pairs = (number_of - 1) // 2
    source_of, receiver = sizes[1:1 + 2 * pairs:2], sizes[2:2 + 2 * pairs:2]
    room = jnp.minimum(source_of - 1, most - receiver)
    moved = jax.random.randint(jax.random.fold_in(rng, 1), (pairs,), 0, 1 << 20) % (room + 1)
    sizes = sizes.at[1:1 + 2 * pairs:2].set(source_of - moved).at[2:2 + 2 * pairs:2].set(receiver + moved)
    return sizes[jax.random.permutation(jax.random.fold_in(rng, 2), number_of)]


def noise(key, dims, deviation, limit, shards=(), held_as=jnp.bfloat16):
    level = steps_of(key, dims, shards, -0.22, 0.18) if shards else 1.0
    drawn = jax.random.normal(key, dims, jnp.float32) * deviation * level
    return jnp.minimum(jnp.maximum(drawn, -limit), limit).astype(held_as)


def setup_inputs(seed: int = 0, part: int = 0) -> dict:
    arg_keys = jax.random.split(jax.random.key(seed), 7)
    part_splits = jax.random.split(jax.random.fold_in(arg_keys[6], part), 7)
    interior_diag = draw_interior_diag(jax.random.fold_in(jax.random.fold_in(arg_keys[6], part), 71), part)
    coupling = noise(part_splits[1], (PARTITIONS * B, B), 0.05, 0.29882812, ((0, 8), (1, 2)))
    arrow_rows = noise(part_splits[2], (PARTITIONS * A, B), 0.1, 0.59765625, ((0, 16),))
    separator_diag = draw_separator_diag(jax.random.fold_in(jax.random.fold_in(arg_keys[6], part), 71), part)
    tip = noise(part_splits[4], (A, A), 1.0, 6.0, ((1, 2),))
    lengths = ragged(part_splits[5], PARTITIONS, PARTITIONS + PARTITIONS // 2, 2, 0).astype(jnp.int32)
    return dict(interior_diag=interior_diag, coupling=coupling, arrow_rows=arrow_rows, separator_diag=separator_diag, tip=tip, lengths=lengths)


def eliminate(operands):
    diag_block, couple, arrows, position, length = operands
    factor = jnp.linalg.cholesky(diag_block.astype(jnp.float32))
    couple = jnp.where(position == 0, jnp.zeros(couple.shape, jnp.float32), couple.astype(jnp.float32))
    right_sides = jnp.concatenate([couple, arrows.astype(jnp.float32).T], axis=1)
    solved = lax.linalg.triangular_solve(factor, right_sides, left_side=True, lower=True).astype(jnp.bfloat16)
    solved = jnp.where(length == 2, solved, jnp.zeros(solved.shape, jnp.bfloat16))
    solved_e = solved[:, :B]
    solved_r = solved[:, B:]
    boundary = jnp.dot(solved_e.T.astype(jnp.float32), solved_e.astype(jnp.float32), preferred_element_type=jnp.float32)
    arrow_term = (-jnp.dot(solved_r.T.astype(jnp.float32), solved_e.astype(jnp.float32), preferred_element_type=jnp.float32)).astype(jnp.bfloat16)
    tip_term = jnp.dot(solved_r.T.astype(jnp.float32), solved_r.astype(jnp.float32), preferred_element_type=jnp.float32)
    return (boundary, arrow_term, tip_term)

def reference(interior_diag, coupling, arrow_rows, separator_diag, tip, lengths):
    positions = jnp.arange(PARTITIONS, dtype=jnp.int32)
    boundary, arrow_term, tip_terms = lax.map(eliminate, (interior_diag.reshape(PARTITIONS, B, B), coupling.reshape(PARTITIONS, B, B), arrow_rows.reshape(PARTITIONS, A, B), positions, lengths.astype(jnp.int32)))
    later_boundary = jnp.concatenate([boundary[1:], jnp.zeros((1, B, B), jnp.float32)], axis=0)
    later_arrow = jnp.concatenate([arrow_term[1:], jnp.zeros((1, A, B), jnp.bfloat16)], axis=0)
    new_separator = (separator_diag.reshape(PARTITIONS, B, B).astype(jnp.float32) - later_boundary).astype(jnp.bfloat16).reshape(PARTITIONS * B, B)
    arrow_fill = later_arrow.reshape(PARTITIONS * A, B)
    new_tip = tip.astype(jnp.float32) - jnp.sum(tip_terms, axis=0)
    return (new_separator, arrow_fill, new_tip)
```

```python
import functools

import jax
import jax.numpy as jnp
from jax import lax
from jax.experimental import pallas as pl
from jax.experimental.pallas import tpu as pltpu
from jax.sharding import PartitionSpec as P

BLOCK = 256
VMEM_LIMIT = 50 * 1024 * 1024


def shifted(block, axis, distance):
    devices = range(lax.axis_size(axis))
    route = [(i - distance, i) for i in devices if i - distance in devices]
    return lax.ppermute(block, axis, route)


def low(x):
    return x.astype(jnp.bfloat16)


def product(a, b):
    return jnp.dot(a, b, preferred_element_type=jnp.float32)


def invert(s, x_ref):
    size = s.shape[0]
    eye = lax.broadcasted_iota(jnp.int32, s.shape, 0) == lax.broadcasted_iota(jnp.int32, s.shape, 1)
    unit = eye.astype(jnp.float32)
    diagonal = jnp.where(eye, s, 0.0)
    row_scale = lax.rsqrt(jnp.sum(diagonal, axis=1, keepdims=True))
    column_scale = lax.rsqrt(jnp.sum(diagonal, axis=0, keepdims=True))
    a = s * row_scale * column_scale
    bound = jnp.max(jnp.sum(jnp.abs(a), axis=0, keepdims=True), axis=1, keepdims=True)
    step = 1.5 / bound
    e = unit - step * a
    e1 = low(e)
    e2 = low(product(e1, e1))
    e4 = low(product(e2, e2))
    x = unit + e
    x = x + product(low(x), e2)
    x = x + product(low(x), e4)
    x_ref[...] = step * x
    a_low = low(a)

    def unfinished(state):
        count, error = state
        return jnp.logical_and(error > 0.01, count < 24)

    def refine(state):
        count, _ = state
        x_low = low(x_ref[...])
        residual = unit - product(a_low, x_low)
        x_ref[...] = x_low.astype(jnp.float32) + product(x_low, low(residual))
        return count + 1, jnp.sum(residual * residual)

    lax.while_loop(unfinished, refine, (jnp.int32(0), jnp.float32(1.0)))
    return x_ref[...] * row_scale * column_scale


def factor_kernel(active_ref, halves_ref, lt_ref, p_ref, d_ref, u_ref, x_ref):
    n = d_ref.shape[0]
    width = halves_ref.shape[1]
    for half in range(n // width):
        d_ref[:, half * width:(half + 1) * width] = halves_ref[half * n:(half + 1) * n, :]
    keep = active_ref[0] == 2
    for k in range(n // BLOCK):
        lo, hi = k * BLOCK, (k + 1) * BLOCK
        row = d_ref[lo:hi, lo:].astype(jnp.float32)
        if k:
            row = row - product(lt_ref[lo:hi, :lo], u_ref[:lo, lo:])
        p = invert(row[:, :BLOCK], x_ref)
        p_low = low(p)
        p_ref[lo:hi, :] = low(jnp.where(keep, p, 0.0))
        lt_ref[lo:hi, lo:hi] = p_low
        if hi < n:
            row_low = low(row[:, BLOCK:])
            u_ref[lo:hi, hi:] = row_low
            lt_ref[lo:hi, hi:] = low(product(p_low, row_low))
            column = d_ref[hi:, lo:hi].astype(jnp.float32)
            if k:
                column = column - product(lt_ref[hi:, :lo], u_ref[:lo, lo:hi])
            lt_ref[hi:, lo:hi] = low(product(low(column), p_low))


def solve_kernel(lt_ref, p_ref, e_ref, r_ref, we_ref, ze_ref, wr_ref, zr_ref, arrow_ref):
    n = lt_ref.shape[0]
    for k in range(n // BLOCK):
        lo, hi = k * BLOCK, (k + 1) * BLOCK
        e = e_ref[lo:hi, :]
        r = r_ref[:, lo:hi]
        if k:
            e = low(e.astype(jnp.float32) - product(lt_ref[lo:hi, :lo], we_ref[:lo, :]))
            r = low(r.astype(jnp.float32) - product(wr_ref[:, :lo], lt_ref[:lo, lo:hi]))
        we_ref[lo:hi, :] = e
        wr_ref[:, lo:hi] = r
        ze_ref[lo:hi, :] = low(product(p_ref[lo:hi, :], e))
        zr_ref[:, lo:hi] = low(product(r, p_ref[lo:hi, :]))
    arrow_ref[...] = low(-product(wr_ref[...], ze_ref[...]))


def in_vmem(count):
    return [pl.BlockSpec(memory_space=pltpu.VMEM)] * count


def shape_of(*dims):
    return jax.ShapeDtypeStruct(dims, jnp.bfloat16)


def factored(length, halves):
    width = halves.shape[1]
    n = halves.shape[0] * width // (halves.shape[0] // 2)
    return pl.pallas_call(
        factor_kernel,
        out_shape=(shape_of(n, n), shape_of(n, BLOCK)),
        in_specs=[pl.BlockSpec(memory_space=pltpu.SMEM)] + in_vmem(1),
        out_specs=tuple(in_vmem(2)),
        scratch_shapes=[
            pltpu.VMEM((n, n), jnp.bfloat16),
            pltpu.VMEM((n, n), jnp.bfloat16),
            pltpu.VMEM((BLOCK, BLOCK), jnp.float32),
        ],
        compiler_params=pltpu.CompilerParams(vmem_limit_bytes=VMEM_LIMIT),
        cost_estimate=pl.CostEstimate(flops=n * n * n, bytes_accessed=4 * n * n, transcendentals=0),
        name="factor",
    )(length, halves)


def eliminated(lt, p, couple, arrows):
    n, columns = couple.shape
    rows = arrows.shape[0]
    return pl.pallas_call(
        solve_kernel,
        out_shape=(
            shape_of(n, columns), shape_of(n, columns),
            shape_of(rows, n), shape_of(rows, n), shape_of(rows, columns),
        ),
        in_specs=in_vmem(4),
        out_specs=tuple(in_vmem(5)),
        compiler_params=pltpu.CompilerParams(vmem_limit_bytes=VMEM_LIMIT),
        cost_estimate=pl.CostEstimate(
            flops=n * n * (columns + rows) + 2 * n * columns * rows,
            bytes_accessed=2 * (n * n + 3 * n * columns + 3 * n * rows),
            transcendentals=0,
        ),
        name="solve",
    )(lt, p, couple, arrows)


def on_device(interior_diag, coupling, arrow_rows, separator_diag, tip, lengths):
    position = lax.axis_index("tm")
    core = lax.axis_index("space")
    halves = lax.all_gather(interior_diag, "space", axis=0, tiled=True)
    arrows = lax.all_gather(arrow_rows, "space", axis=0, tiled=True)
    length = lax.dynamic_slice(lengths, (position,), (1,))
    lt, p = factored(length, halves)
    we, ze, wr, zr, own_arrow = eliminated(lt, p, coupling, arrows)
    arrow_fill = shifted(own_arrow, "tm", -1)

    other_ze = lax.ppermute(ze, "space", [(0, 1), (1, 0)])
    first = core == 0
    width = coupling.shape[1]
    part = width // 2
    left = jnp.where(first, we[:, :part], other_ze[:, part:])
    right = jnp.where(first, other_ze, we)
    cross = low(jnp.einsum("kb,kc->bc", left, right, preferred_element_type=jnp.float32))
    cross = shifted(cross, "tm", -1)
    own = low(jnp.einsum("kb,kc->bc", we, ze, preferred_element_type=jnp.float32))
    own = shifted(own, "tm", -1)
    cross = lax.all_gather(cross, "space", axis=0, tiled=True)

    tip_width = tip.shape[1]
    zr_own = lax.dynamic_slice(zr, (core * tip_width, 0), (tip_width, zr.shape[1]))
    tip_term = jnp.einsum("ak,ck->ac", wr, zr_own, preferred_element_type=jnp.float32)
    new_tip = tip.astype(jnp.float32) - lax.psum(tip_term, "tm")

    separator = separator_diag.astype(jnp.float32)
    top = jnp.where(first, own, cross).astype(jnp.float32)
    bottom = jnp.where(first, cross.T, own).astype(jnp.float32)
    new_separator = low(separator - jnp.concatenate([top, bottom], axis=0))
    return (new_separator, arrow_fill, new_tip)


def solution(mesh):
    return jax.shard_map(
        on_device,
        mesh=mesh,
        in_specs=(
            P(("groups", "tm"), "space"),
            P(("groups", "tm"), "space"),
            P(("groups", "tm", "space"), None),
            P(("groups", "tm"), "space"),
            P("groups", "space"),
            P("groups"),
        ),
        out_specs=(
            P(("groups", "tm"), "space"),
            P(("groups", "tm"), "space"),
            P("groups", "space"),
        ),
        check_vma=False,
    )
```

```python
import functools

import jax
import jax.numpy as jnp
from jax import lax
from jax.experimental import pallas as pl
from jax.experimental.pallas import tpu as pltpu
from jax.sharding import PartitionSpec as P

BLOCK = 256
VMEM_LIMIT = 50 * 1024 * 1024


def shifted(block, axis, distance):
    devices = range(lax.axis_size(axis))
    route = [(i - distance, i) for i in devices if i - distance in devices]
    return lax.ppermute(block, axis, route)


def low(x):
    return x.astype(jnp.bfloat16)


def product(a, b):
    return jnp.dot(a, b, preferred_element_type=jnp.float32)


def invert(s, x_ref):
    size = s.shape[0]
    eye = lax.broadcasted_iota(jnp.int32, s.shape, 0) == lax.broadcasted_iota(jnp.int32, s.shape, 1)
    unit = eye.astype(jnp.float32)
    diagonal = jnp.where(eye, s, 0.0)
    row_scale = lax.rsqrt(jnp.sum(diagonal, axis=1, keepdims=True))
    column_scale = lax.rsqrt(jnp.sum(diagonal, axis=0, keepdims=True))
    a = s * row_scale * column_scale
    bound = jnp.max(jnp.sum(jnp.abs(a), axis=0, keepdims=True), axis=1, keepdims=True)
    step = 1.5 / bound
    e = unit - step * a
    e1 = low(e)
    e2 = low(product(e1, e1))
    e4 = low(product(e2, e2))
    x = unit + e
    x = x + product(low(x), e2)
    x = x + product(low(x), e4)
    x_ref[...] = step * x
    a_low = low(a)

    def unfinished(state):
        count, error = state
        return jnp.logical_and(error > 0.01, count < 24)

    def refine(state):
        count, _ = state
        x_low = low(x_ref[...])
        residual = unit - product(a_low, x_low)
        x_ref[...] = x_low.astype(jnp.float32) + product(x_low, low(residual))
        return count + 1, jnp.sum(residual * residual)

    lax.while_loop(unfinished, refine, (jnp.int32(0), jnp.float32(1.0)))
    return x_ref[...] * row_scale * column_scale


def factor_kernel(case_ref, own_ref, other_ref, lt_ref, p_ref, d_ref, u_ref, x_ref):
    n, width = own_ref.shape
    first = case_ref[1] == 0
    for lo in range(0, n, BLOCK):
        rows = slice(lo, lo + BLOCK)
        own, other = own_ref[rows, :], other_ref[rows, :]
        d_ref[rows, :width] = jnp.where(first, own, other)
        d_ref[rows, width:] = jnp.where(first, other, own)
    keep = case_ref[0] == 2
    for k in range(n // BLOCK):
        lo, hi = k * BLOCK, (k + 1) * BLOCK
        row = d_ref[lo:hi, lo:].astype(jnp.float32)
        if k:
            row = row - product(lt_ref[lo:hi, :lo], u_ref[:lo, lo:])
        p = invert(row[:, :BLOCK], x_ref)
        p_low = low(p)
        p_ref[lo:hi, :] = low(jnp.where(keep, p, 0.0))
        lt_ref[lo:hi, lo:hi] = p_low
        if hi < n:
            row_low = low(row[:, BLOCK:])
            u_ref[lo:hi, hi:] = row_low
            lt_ref[lo:hi, hi:] = low(product(p_low, row_low))
            column = d_ref[hi:, lo:hi].astype(jnp.float32)
            if k:
                column = column - product(lt_ref[hi:, :lo], u_ref[:lo, lo:hi])
            lt_ref[hi:, lo:hi] = low(product(low(column), p_low))


def arrow_kernel(case_ref, lt_ref, p_ref, r_ref, wr_ref, tip_ref, z_ref):
    n = lt_ref.shape[0]
    width = tip_ref.shape[1]
    mine = pl.ds(pl.multiple_of(case_ref[1] * width, width), width)
    for k in range(n // BLOCK):
        lo, hi = k * BLOCK, (k + 1) * BLOCK
        r = r_ref[:, lo:hi]
        if k:
            r = low(r.astype(jnp.float32) - product(wr_ref[:, :lo], lt_ref[:lo, lo:hi]))
        wr_ref[:, lo:hi] = r
        z_ref[:, lo:hi] = low(product(wr_ref[mine, lo:hi], p_ref[lo:hi, :]))
    tip_ref[...] = low(lax.dot_general(
        wr_ref[...], z_ref[...], (((1,), (1,)), ((), ())), preferred_element_type=jnp.float32
    ))


def solve_kernel(lt_ref, p_ref, e_ref, wr_ref, we_ref, ze_ref, arrow_ref):
    n = lt_ref.shape[0]
    for k in range(n // BLOCK):
        lo, hi = k * BLOCK, (k + 1) * BLOCK
        e = e_ref[lo:hi, :]
        if k:
            e = low(e.astype(jnp.float32) - product(lt_ref[lo:hi, :lo], we_ref[:lo, :]))
        we_ref[lo:hi, :] = e
        ze_ref[lo:hi, :] = low(product(p_ref[lo:hi, :], e))
    arrow_ref[...] = low(-product(wr_ref[...], ze_ref[...]))


def in_vmem(count):
    return [pl.BlockSpec(memory_space=pltpu.VMEM)] * count


def shape_of(*dims):
    return jax.ShapeDtypeStruct(dims, jnp.bfloat16)


def in_smem():
    return [pl.BlockSpec(memory_space=pltpu.SMEM)]


def factored(case, own, other):
    n = own.shape[0]
    return pl.pallas_call(
        factor_kernel,
        out_shape=(shape_of(n, n), shape_of(n, BLOCK)),
        in_specs=in_smem() + in_vmem(2),
        out_specs=tuple(in_vmem(2)),
        scratch_shapes=[
            pltpu.VMEM((n, n), jnp.bfloat16),
            pltpu.VMEM((n, n), jnp.bfloat16),
            pltpu.VMEM((BLOCK, BLOCK), jnp.float32),
        ],
        compiler_params=pltpu.CompilerParams(vmem_limit_bytes=VMEM_LIMIT),
        cost_estimate=pl.CostEstimate(flops=5 * n * n * n, bytes_accessed=4 * n * n, transcendentals=0),
        name="factor",
    )(case, own, other)


def arrow_terms(case, lt, p, arrows, tip_width):
    rows, n = arrows.shape
    return pl.pallas_call(
        arrow_kernel,
        out_shape=(shape_of(rows, n), shape_of(rows, tip_width)),
        in_specs=in_smem() + in_vmem(3),
        out_specs=tuple(in_vmem(2)),
        scratch_shapes=[pltpu.VMEM((tip_width, n), jnp.bfloat16)],
        compiler_params=pltpu.CompilerParams(vmem_limit_bytes=VMEM_LIMIT),
        cost_estimate=pl.CostEstimate(
            flops=n * n * rows + 2 * n * rows * tip_width,
            bytes_accessed=2 * (n * n + 2 * n * rows),
            transcendentals=0,
        ),
        name="arrow",
    )(case, lt, p, arrows)


def eliminated(lt, p, couple, wr):
    n, columns = couple.shape
    rows = wr.shape[0]
    return pl.pallas_call(
        solve_kernel,
        out_shape=(shape_of(n, columns), shape_of(n, columns), shape_of(rows, columns)),
        in_specs=in_vmem(4),
        out_specs=tuple(in_vmem(3)),
        compiler_params=pltpu.CompilerParams(vmem_limit_bytes=VMEM_LIMIT),
        cost_estimate=pl.CostEstimate(
            flops=n * n * columns + 2 * n * columns * rows,
            bytes_accessed=2 * (n * n + 3 * n * columns + n * rows),
            transcendentals=0,
        ),
        name="solve",
    )(lt, p, couple, wr)


def swapped(block):
    return lax.ppermute(block, "space", [(0, 1), (1, 0)])


def on_device(interior_diag, coupling, arrow_rows, separator_diag, tip, lengths):
    position = lax.axis_index("tm")
    core = lax.axis_index("space")
    first = core == 0
    other_diag = swapped(interior_diag)
    arrow_rows, other_diag = lax.optimization_barrier((arrow_rows, other_diag))
    arrows = lax.all_gather(arrow_rows, "space", axis=0, tiled=True)
    length = lax.dynamic_slice(lengths, (position,), (1,))
    case = jnp.concatenate([length, core.astype(length.dtype)[None]])
    lt, p = factored(case, interior_diag, other_diag)

    wr, tip_term = arrow_terms(case, lt, p, arrows, tip.shape[1])
    tip_sum = lax.psum(tip_term, "tm")

    we, ze, own_arrow = eliminated(lt, p, coupling, wr)
    arrow_fill = shifted(own_arrow, "tm", -1)
    other_ze = swapped(ze)
    own = low(jnp.einsum("kb,kc->bc", we, ze, preferred_element_type=jnp.float32))
    own, other_ze, tip_sum = lax.optimization_barrier((own, other_ze, tip_sum))
    own = shifted(own, "tm", -1)

    width = coupling.shape[1]
    part = width // 2
    left = jnp.where(first, we[:, :part], other_ze[:, part:])
    right = jnp.where(first, other_ze, we)
    cross = low(jnp.einsum("kb,kc->bc", left, right, preferred_element_type=jnp.float32))
    cross = shifted(cross, "tm", -1)
    cross = lax.all_gather(cross, "space", axis=0, tiled=True)
    cross = jnp.where(first, cross.T, cross)

    halves = separator_diag.reshape(2, width, width)
    mine = lax.broadcasted_iota(jnp.int32, halves.shape, 0) == core
    crossed = low(halves.astype(jnp.float32) - cross.astype(jnp.float32)[None])
    crossed = jnp.where(mine, halves, crossed)
    crossed, own = lax.optimization_barrier((crossed, own))
    result = crossed.astype(jnp.float32) - jnp.where(mine, own.astype(jnp.float32)[None], 0.0)
    new_separator = low(result).reshape(separator_diag.shape)
    new_tip = tip.astype(jnp.float32) - tip_sum.astype(jnp.float32)
    return (new_separator, arrow_fill, new_tip)


def solution(mesh):
    return jax.shard_map(
        on_device,
        mesh=mesh,
        in_specs=(
            P(("groups", "tm"), "space"),
            P(("groups", "tm"), "space"),
            P(("groups", "tm", "space"), None),
            P(("groups", "tm"), "space"),
            P("groups", "space"),
            P("groups"),
        ),
        out_specs=(
            P(("groups", "tm"), "space"),
            P(("groups", "tm"), "space"),
            P("groups", "space"),
        ),
        check_vma=False,
    )
```
